32 devices in a mesh: img: 16 (over z, y, x), rep: 2 (over core).
Axes of the slice: x: 2, y: 2, z: 4, core: 2. Of those that a mesh axis runs over, the one named last changes fastest.
Arguments:
- panels: float32 [32, 512, 128], P('img', 'rep'), may hold values from -6 to 6
- blocks: bfloat16 [768, 512, 512], P('img', None, 'rep'), may hold values from -0.25 to 0.25
- pairs: int32 [768, 2], P('img'), may hold values from 0 to 31, as said below
- counts: int32 [16], P('img'), may hold values from 12 to 48, as said below
Outputs:
- basis: float32 [32, 512, 128], P('img', 'rep')
The draws below stay inside these ranges and needn't reach their ends.
Inputs may be any that keep to these rules, and one draw needn't show every extreme that they name: `pairs`: row d * 48 + s is slot s of index d of img: its first image is one of d * 2 to d * 2 + 1, its second image lies on one of the indices d + 1 to d + 8 modulo 16. At most 6 slots of one index name second images on one other index, and that many is reached. `counts`: some index of img has all 48 slots live.
All inputs are finite; a program needn't handle non-finite values.
Results may differ from the reference program's by a relative error of at most 0.0025.
The reference program's roundings to bfloat16 on the way (of `rounded` and `reverse`) count: a program that leaves them out, or rounds other values in their place, can miss the bound.
Values may be sent and summed in bfloat16 or wider, within the bound.
No kernel may reach another device: no remote copies, remote signals or barrier semaphores. Data moves between devices by JAX's collectives and lax.ppermute only.
A program may use at most 128 MiB of HBM per device.

```python
import jax
import jax.numpy as jnp
from jax import lax

KEYPTS = 512
UNIV = 128
BAND = 8
IMG_DEV = 2
PAIR_DEV = 48
IMAGES = 32
PAIRS = 768
N_IMG = 16


def draw_pairs(key, part):
    base = jax.random.fold_in(key, 17)
    order_key, first_key, second_key = jax.random.split(base, 3)
    orders = jax.vmap(lambda single: jax.random.permutation(single, BAND))(jax.random.split(order_key, N_IMG))
    slot_ids = jnp.arange(PAIR_DEV) % BAND
    device_ids = jnp.arange(N_IMG)[:, None]
    peers = (device_ids + 1 + orders[:, slot_ids]) % N_IMG
    first = device_ids * IMG_DEV + jax.random.randint(first_key, (N_IMG, PAIR_DEV), 0, IMG_DEV)
    second = peers * IMG_DEV + jax.random.randint(second_key, (N_IMG, PAIR_DEV), 0, IMG_DEV)
    return jnp.stack([first, second], axis=-1).reshape(N_IMG * PAIR_DEV, 2).astype(jnp.int32)


def draw_counts(key, part):
    base = jax.random.fold_in(key, 29)
    count_key, pick_key = jax.random.split(base, 2)
    drawn = jax.random.randint(count_key, (N_IMG,), PAIR_DEV // 4, PAIR_DEV + 1)
    chosen = jax.random.randint(pick_key, (), 0, N_IMG)
    drawn = jnp.where(jnp.arange(N_IMG) == chosen, PAIR_DEV, drawn)
    return drawn.astype(jnp.int32)


def levels(rng, dims, cuts, low, high):
    gain = 1.0
    for position, blocks in cuts:
        draws = jax.random.uniform(jax.random.fold_in(jax.random.fold_in(rng, 6), position), (blocks,), jnp.float32, low / len(cuts), high / len(cuts))
        gain = gain * jnp.repeat(jnp.exp(draws), dims[position] // blocks).reshape((-1,) + (1,) * (len(dims) - 1 - position))
    return gain


def gaussian(rng, extent, scale, limit, shards=(), kind=jnp.bfloat16):
    values = jax.random.normal(rng, extent, jnp.float32) * scale
    if len(shards) > 0:
        values = levels(rng, extent, shards, -0.22, 0.18) * values
    return jnp.clip(values, min=-limit, max=limit).astype(kind)


def setup_inputs(seed: int = 0) -> dict:
    keys = jax.random.split(jax.random.key(seed), 5)
    return {
        "panels": gaussian(keys[0], (IMAGES, KEYPTS, UNIV), 1.0, 6.0, ((0, 16), (1, 2)), jnp.float32),
        "blocks": gaussian(keys[1], (PAIRS, KEYPTS, KEYPTS), KEYPTS ** -0.5, 0.25, ((0, 16), (2, 2))),
        "pairs": draw_pairs(jax.random.fold_in(keys[4], 71), 0),
        "counts": draw_counts(jax.random.fold_in(keys[4], 71), 0),
    }


def reference(panels, blocks, pairs, counts):
    rounded = panels.astype(jnp.bfloat16)
    images_all = IMG_DEV * N_IMG
    slot_ids = jnp.arange(PAIR_DEV)

    def one_device(field, device):
        block_rows = lax.dynamic_slice_in_dim(blocks, device * PAIR_DEV, PAIR_DEV, 0).astype(jnp.float32)
        pair_rows = lax.dynamic_slice_in_dim(pairs, device * PAIR_DEV, PAIR_DEV, 0)
        alive_mask = (slot_ids < counts[device]).astype(jnp.float32)
        second_panels = rounded[pair_rows[:, 1]].astype(jnp.float32)
        first_panels = rounded[pair_rows[:, 0]].astype(jnp.float32)
        forward = jnp.einsum('skl,sln->skn', block_rows, second_panels)
        reverse = jnp.einsum('skl,skn->sln', block_rows, first_panels).astype(jnp.bfloat16)
        reverse = lax.optimization_barrier(reverse).astype(jnp.float32)
        field = field.at[pair_rows[:, 0]].add(forward * alive_mask[:, None, None])
        field = field.at[pair_rows[:, 1]].add(reverse * alive_mask[:, None, None])
        return (field, None)
    start_field = jnp.zeros((images_all, KEYPTS, UNIV), jnp.float32)
    field, _ = lax.scan(one_device, start_field, jnp.arange(N_IMG))
    field = panels + field
    gram_matrix = jnp.einsum('ikn,ikm->nm', field.astype(jnp.float32), field.astype(jnp.float32), precision=lax.Precision.HIGHEST, preferred_element_type=jnp.float32)
    gram_matrix = gram_matrix / (images_all * KEYPTS)
    factor = jnp.linalg.cholesky(gram_matrix)
    stacked = field.reshape(images_all * KEYPTS, UNIV)
    basis = lax.linalg.triangular_solve(factor, stacked, left_side=False, lower=True, transpose_a=True)
    return basis.reshape(images_all, KEYPTS, UNIV)
```

```python
import functools

import jax
import jax.numpy as jnp
from jax import lax
from jax.experimental import pallas as pl
from jax.experimental.pallas import tpu as pltpu
from jax.sharding import PartitionSpec as P

BAND = 8
GROUP = BAND // 2
SMEM = pl.BlockSpec(memory_space=pltpu.SMEM)
VMEM = pl.BlockSpec(memory_space=pltpu.VMEM)


def passed_along(value, axis, steps):
    count = lax.axis_size(axis)
    pairs = [(source, (source + steps) % count) for source in range(count)]
    return lax.ppermute(value, axis, pairs)


def exchanged(value, axis, bits):
    count = lax.axis_size(axis)
    return lax.ppermute(value, axis, [(source, source ^ bits) for source in range(count)])


def entry(second, own_index, devices, img_dev):
    owner = lax.div(second, img_dev)
    image = second - owner * img_dev
    member = lax.rem(owner, GROUP)
    own_member = lax.rem(own_index, GROUP)
    groups = devices // GROUP
    hop = lax.rem(lax.div(owner, GROUP) - lax.div(own_index, GROUP) + groups, groups)
    turn = hop - jnp.where(member <= own_member, 1, 0)
    return ((member ^ own_member) * 2 + turn) * img_dev + image


def reverse_kernel(per, devices, place, count, pairs, near, far, blocks, *rest):
    outs, (turned, total) = rest[:GROUP], rest[GROUP:]
    own_index, core = place[0], place[1]
    img_dev, half = near.shape[0], near.shape[1]
    units = 2 * img_dev
    near_rows = pl.ds(pl.multiple_of(core * half, half), half)
    far_rows = pl.ds(pl.multiple_of((1 - core) * half, half), half)
    for image in range(img_dev):
        turned[0, image] = near[image].T
        turned[1, image] = far[image].T
    total[...] = jnp.zeros_like(total)

    @pl.loop(0, (count[0] + per - 1) // per)
    def _(step):
        for part in range(per):
            slot = step * per + part
            place_in = entry(pairs[slot, 1], own_index, devices, img_dev)
            place_in = jnp.where(slot < count[0], place_in, GROUP * units)
            first = pairs[slot, 0] - own_index * img_dev
            product = jnp.dot(
                turned[0, first], blocks[slot, near_rows], preferred_element_type=jnp.float32
            )
            product += jnp.dot(
                turned[1, first], blocks[slot, far_rows], preferred_element_type=jnp.float32
            )
            total[place_in] += product.astype(jnp.bfloat16).astype(jnp.float32)

    for member in range(GROUP):
        for unit in range(units):
            outs[member][unit] = total[member * units + unit].astype(jnp.bfloat16).T


def forward_kernel(per, devices, place, count, pairs, panels, *rest):
    tables, blocks, own, send, table, total = rest[:GROUP], *rest[GROUP:]
    own_index, core = place[0], place[1]
    img_dev, half = panels.shape[0], panels.shape[1]
    units = 2 * img_dev
    for member in range(GROUP):
        table[pl.ds(member * units, units)] = tables[member][...]
    total[...] = jnp.zeros_like(total)

    @pl.loop(0, (count[0] + per - 1) // per)
    def _(step):
        for part in range(per):
            slot = step * per + part
            place_in = entry(pairs[slot, 1], own_index, devices, img_dev)
            place_in = jnp.clip(place_in, 0, GROUP * units - 1)
            first = pairs[slot, 0] - own_index * img_dev
            first = jnp.where(slot < count[0], first, img_dev)
            total[first] += jnp.dot(
                blocks[slot], table[place_in], preferred_element_type=jnp.float32
            )

    for image in range(img_dev):
        near_rows = pl.ds(pl.multiple_of(core * half, half), half)
        far_rows = pl.ds(pl.multiple_of((1 - core) * half, half), half)
        own[image] = panels[image] + total[image, near_rows]
        send[image] = total[image, far_rows]


def shards(panels, blocks, pairs, counts):
    devices = lax.axis_size("img")
    own_index = lax.axis_index("img")
    core = lax.axis_index("rep")
    member = own_index % GROUP
    img_dev, half, univ = panels.shape
    slots, keypts, cols = blocks.shape
    units = 2 * img_dev
    per = next(width for width in (8, 6, 4, 3, 2, 1) if slots % width == 0)
    place = jnp.stack([own_index, core]).astype(jnp.int32)
    limit = pltpu.CompilerParams(vmem_limit_bytes=40 << 20)
    work = pl.CostEstimate(
        flops=2 * slots * keypts * cols * univ,
        bytes_accessed=slots * keypts * cols * 2,
        transcendentals=0,
    )

    near = panels.astype(jnp.bfloat16)
    far = exchanged(near, "rep", 1)
    ahead = [near, passed_along(near, "img", -GROUP), passed_along(near, "img", -2 * GROUP)]

    returns = pl.pallas_call(
        functools.partial(reverse_kernel, per, devices),
        in_specs=[SMEM] * 3 + [VMEM] * 3,
        out_specs=[VMEM] * GROUP,
        out_shape=[jax.ShapeDtypeStruct((units, cols, univ), jnp.bfloat16)] * GROUP,
        scratch_shapes=[
            pltpu.VMEM((2, img_dev, univ, half), jnp.bfloat16),
            pltpu.VMEM((GROUP * units + 1, univ, cols), jnp.float32),
        ],
        compiler_params=limit,
        cost_estimate=work,
        name="reverse",
    )(place, counts, pairs, near, far, blocks)

    tables = [jnp.concatenate(ahead[1:])]
    for bits in range(1, GROUP):
        later = member > (member ^ bits)
        sent = jnp.where(later, jnp.concatenate(ahead[:2]), jnp.concatenate(ahead[1:]))
        tables.append(exchanged(sent, "img", bits))

    arrived = [returns[0]] + [exchanged(returns[bits], "img", bits) for bits in range(1, GROUP)]
    sums = [jnp.zeros((img_dev, cols, univ), jnp.float32) for _ in range(3)]
    for bits in range(GROUP):
        first_unit = arrived[bits][:img_dev].astype(jnp.float32)
        second_unit = arrived[bits][img_dev:].astype(jnp.float32)
        earlier = (member ^ bits) < member
        sums[0] += jnp.where(earlier, first_unit, 0)
        sums[1] += jnp.where(earlier, second_unit, first_unit)
        sums[2] += jnp.where(earlier, 0, second_unit)
    back = [
        passed_along(sums[hop].astype(jnp.bfloat16), "img", hop * GROUP) for hop in (1, 2)
    ]

    own, send = pl.pallas_call(
        functools.partial(forward_kernel, per, devices),
        in_specs=[SMEM] * 3 + [VMEM] * (GROUP + 2),
        out_specs=[VMEM] * 2,
        out_shape=[jax.ShapeDtypeStruct((img_dev, half, univ), jnp.float32)] * 2,
        scratch_shapes=[
            pltpu.VMEM((GROUP * units, cols, univ), jnp.bfloat16),
            pltpu.VMEM((img_dev + 1, keypts, univ), jnp.float32),
        ],
        compiler_params=limit,
        cost_estimate=work,
        name="forward",
    )(place, counts, pairs, panels, *tables, blocks)
    other_half = exchanged(send, "rep", 1)

    field = own + other_half + sums[0] + back[0].astype(jnp.float32) + back[1].astype(jnp.float32)
    gram = jnp.einsum(
        "ikn,ikm->nm",
        field,
        field,
        precision=lax.Precision.HIGHEST,
        preferred_element_type=jnp.float32,
    )
    gram = gram + exchanged(gram, "rep", 1)
    bits = 1
    while bits < devices:
        gram = gram + exchanged(gram, "img", bits)
        bits *= 2
    gram = gram / (devices * img_dev * keypts)
    factor = jnp.linalg.cholesky(gram)
    stacked = field.reshape(img_dev * half, univ)
    basis = lax.linalg.triangular_solve(
        factor, stacked, left_side=False, lower=True, transpose_a=True
    )
    return basis.reshape(img_dev, half, univ)


def solution(mesh):
    in_specs = (P("img", "rep", None), P("img", None, "rep"), P("img", None), P("img"))
    out_specs = P("img", "rep", None)
    return jax.shard_map(shards, mesh=mesh, in_specs=in_specs, out_specs=out_specs, check_vma=False)
```

```python
import functools

import jax
import jax.numpy as jnp
from jax import lax
from jax.experimental import pallas as pl
from jax.experimental.pallas import tpu as pltpu
from jax.sharding import PartitionSpec as P

BAND = 8
GROUP = BAND // 2
ROWS = 8
SMEM = pl.BlockSpec(memory_space=pltpu.SMEM)
VMEM = pl.BlockSpec(memory_space=pltpu.VMEM)
SHORT = pl.CostEstimate(flops=1, bytes_accessed=1, transcendentals=0)
LONG = pl.CostEstimate(flops=10**11, bytes_accessed=10**8, transcendentals=0)
LIMIT = pltpu.CompilerParams(vmem_limit_bytes=53 << 20)


def passed_along(value, axis, steps):
    count = lax.axis_size(axis)
    pairs = [(source, (source + steps) % count) for source in range(count)]
    return lax.ppermute(value, axis, pairs)


def exchanged(value, axis, bits):
    count = lax.axis_size(axis)
    return lax.ppermute(value, axis, [(source, source ^ bits) for source in range(count)])


def entry(second, own_index, devices, img_dev):
    owner = lax.div(second, img_dev)
    member = lax.rem(owner, GROUP)
    own_member = lax.rem(own_index, GROUP)
    groups = devices // GROUP
    hop = lax.rem(lax.div(owner, GROUP) - lax.div(own_index, GROUP) + groups, groups)
    turn = hop - jnp.where(member <= own_member, 1, 0)
    return ((member ^ own_member) * 2 + turn) * img_dev + second - owner * img_dev


def reverse_kernel(per, devices, place, count, pairs, near, far, blocks, *rest):
    outs, (kept, turned, total, landed) = rest[:GROUP], rest[GROUP:]
    core, own_index = place[0], place[1]
    img_dev, half = near.shape[0], near.shape[1]
    units = 2 * img_dev
    steps = blocks.shape[0] // per

    def fetch(step):
        rows = pl.ds(step * per, per)
        return pltpu.make_async_copy(blocks.at[rows], kept.at[rows], landed.at[step])

    for step in range(steps):
        fetch(step).start()
    near_columns = pl.ds(pl.multiple_of(core * half, half), half)
    far_columns = pl.ds(pl.multiple_of((1 - core) * half, half), half)
    for image in range(img_dev):
        turned[image, :, near_columns] = near[image].T
        turned[image, :, far_columns] = far[image].T
    total[...] = jnp.zeros_like(total)

    @pl.loop(0, steps)
    def _(step):
        fetch(step).wait()
        for part in range(per):
            slot = step * per + part
            place_in = entry(pairs[slot, 1], own_index, devices, img_dev)
            place_in = jnp.where(slot < count[0], place_in, GROUP * units)
            first = pairs[slot, 0] - own_index * img_dev
            product = jnp.dot(turned[first], kept[slot], preferred_element_type=jnp.float32)
            total[place_in] += product.astype(jnp.bfloat16).astype(jnp.float32)

    for member in range(GROUP):
        for unit in range(units):
            outs[member][unit] = total[member * units + unit].astype(jnp.bfloat16).T


def forward_kernel(per, devices, place, count, pairs, panels, blocks, *rest):
    tables, (own, send, kept, table, total, landed) = rest[:GROUP], rest[GROUP:]
    core, own_index = place[0], place[1]
    img_dev, half = panels.shape[0], panels.shape[1]
    units = 2 * img_dev
    steps = blocks.shape[0] // per

    def fetch(step):
        rows = pl.ds(step * per, per)
        return pltpu.make_async_copy(blocks.at[rows], kept.at[rows], landed.at[step])

    for step in range(steps):
        fetch(step).start()
    for member in range(GROUP):
        table[pl.ds(member * units, units)] = tables[member][...]
    total[...] = jnp.zeros_like(total)

    @pl.loop(0, steps)
    def _(step):
        fetch(step).wait()
        for part in range(per):
            slot = step * per + part
            place_in = entry(pairs[slot, 1], own_index, devices, img_dev)
            place_in = jnp.clip(place_in, 0, GROUP * units - 1)
            first = pairs[slot, 0] - own_index * img_dev
            first = jnp.where(slot < count[0], first, img_dev)
            total[first] += jnp.dot(
                kept[slot], table[place_in], preferred_element_type=jnp.float32
            )

    near_rows = pl.ds(pl.multiple_of(core * half, half), half)
    far_rows = pl.ds(pl.multiple_of((1 - core) * half, half), half)
    for image in range(img_dev):
        own[image] = panels[image] + total[image, near_rows]
        send[image] = total[image, far_rows]


def gram_kernel(own, other, near_sum, back_one, back_two, field, packed):
    univ = packed.shape[1]
    gram = jnp.zeros((univ, univ), jnp.float32)
    for image in range(field.shape[0]):
        rows = own[image] + other[image] + near_sum[image]
        rows += back_one[image].astype(jnp.float32) + back_two[image].astype(jnp.float32)
        field[image] = rows
        gram += lax.dot_general(
            rows,
            rows,
            (((0,), (0,)), ((), ())),
            precision=lax.Precision.HIGHEST,
            preferred_element_type=jnp.float32,
        )
    side = univ // 2
    row_ids = lax.broadcasted_iota(jnp.int32, (side, side), 0)
    column_ids = lax.broadcasted_iota(jnp.int32, (side, side), 1)
    last = gram[side:, side:]
    mixed = jnp.where(row_ids <= column_ids, gram[:side, :side], last)
    packed[pl.ds(0, side), :] = jnp.concatenate([mixed, gram[:side, side:]], axis=1)
    diagonal = jnp.sum(jnp.where(row_ids == column_ids, last, 0.0), axis=0, keepdims=True)
    diagonal = jnp.concatenate([diagonal, diagonal], axis=1)
    packed[pl.ds(side, ROWS), :] = jnp.broadcast_to(diagonal, (ROWS, univ))


def solve_kernel(scale, terms, *rest):
    packs, (field, basis, inverse) = rest[:terms], rest[terms:]
    univ = inverse.shape[0]
    side = univ // 2
    packed = packs[0][...]
    for pack in packs[1:]:
        packed += pack[...]
    packed *= scale
    row_ids = lax.broadcasted_iota(jnp.int32, (side, side), 0)
    column_ids = lax.broadcasted_iota(jnp.int32, (side, side), 1)
    mixed = packed[:side, :side]
    turned = mixed.T
    head = jnp.where(row_ids <= column_ids, mixed, turned)
    last = jnp.where(row_ids > column_ids, mixed, turned)
    diagonal = jnp.broadcast_to(packed[side : side + 1, :side], (side, side))
    last = jnp.where(row_ids == column_ids, diagonal, last)
    inverse[pl.ds(0, side), :] = jnp.concatenate([head, packed[:side, side:]], axis=1)
    inverse[pl.ds(side, side), :] = jnp.concatenate([last, last], axis=1)

    count = univ // ROWS
    shape = (ROWS, univ)
    row_ids = lax.broadcasted_iota(jnp.int32, shape, 0)
    column_ids = lax.broadcasted_iota(jnp.int32, shape, 1)
    left = [inverse[pl.ds(b * ROWS, ROWS), :] for b in range(count)]
    right = [
        jnp.where(column_ids == row_ids + b * ROWS, 1.0, 0.0).astype(jnp.float32)
        for b in range(count)
    ]

    def spread(value, row):
        return jnp.broadcast_to(value[row : row + 1, :], shape)

    for b in range(count):
        rows, tail = left[b], right[b]
        columns = [
            jnp.broadcast_to(rows[:, b * ROWS + j : b * ROWS + j + 1], shape) for j in range(ROWS)
        ]
        pivots = jnp.ones(shape, jnp.float32)
        for j in range(ROWS):
            pivot = spread(columns[j], j)
            pivots = jnp.where(row_ids == j, pivot, pivots)
            if j < ROWS - 1:
                weight = jnp.where(row_ids > j, columns[j] * (1.0 / pivot), 0.0)
                for k in range(j + 1, ROWS):
                    columns[k] = columns[k] - weight * spread(columns[k], j)
                rows = rows - weight * spread(rows, j)
                tail = tail - weight * spread(tail, j)
        inverse[pl.ds(b * ROWS, ROWS), :] = tail * lax.rsqrt(pivots)
        if b < count - 1:
            turned = (rows * (1.0 / pivots)).T
            for c in range(b + 1, count):
                for j in range(ROWS):
                    weight = jnp.broadcast_to(turned[c * ROWS : (c + 1) * ROWS, j : j + 1], shape)
                    left[c] = left[c] - weight * spread(rows, j)
                    right[c] = right[c] - weight * spread(tail, j)
    for image in range(field.shape[0]):
        basis[image] = lax.dot_general(
            field[image],
            inverse[...],
            (((1,), (1,)), ((), ())),
            precision=lax.Precision.HIGHEST,
            preferred_element_type=jnp.float32,
        )


def shards(panels, blocks, pairs, counts):
    devices = lax.axis_size("img")
    own_index = lax.axis_index("img")
    member = own_index % GROUP
    img_dev, half, univ = panels.shape
    slots, keypts, cols = blocks.shape
    units = 2 * img_dev
    per = next(width for width in (8, 6, 4, 3, 2, 1) if slots % width == 0)
    place = jnp.stack([lax.axis_index("rep"), own_index]).astype(jnp.int32)
    anywhere = pl.BlockSpec(memory_space=pl.ANY)

    near = panels.astype(jnp.bfloat16)
    far = exchanged(near, "rep", 1)
    returns = pl.pallas_call(
        functools.partial(reverse_kernel, per, devices),
        in_specs=[SMEM] * 3 + [VMEM] * 2 + [anywhere],
        out_specs=[VMEM] * GROUP,
        out_shape=[jax.ShapeDtypeStruct((units, cols, univ), jnp.bfloat16)] * GROUP,
        scratch_shapes=[
            pltpu.VMEM(blocks.shape, blocks.dtype),
            pltpu.VMEM((img_dev, univ, keypts), jnp.bfloat16),
            pltpu.VMEM((GROUP * units + 1, univ, cols), jnp.float32),
            pltpu.SemaphoreType.DMA((slots // per,)),
        ],
        compiler_params=LIMIT,
        cost_estimate=SHORT,
        name="reverse",
    )(place, counts, pairs, near, far, blocks)

    arrived = [exchanged(returns[bits], "img", bits) for bits in range(1, GROUP)]
    part = (img_dev, cols, univ)
    sums = [jnp.zeros(part, jnp.float32) for _ in range(3)]
    for bits, value in enumerate([returns[0]] + arrived):
        first_unit = value[:img_dev].astype(jnp.float32)
        second_unit = value[img_dev:].astype(jnp.float32)
        earlier = (member ^ bits) < member
        sums[0] += jnp.where(earlier, first_unit, 0)
        sums[1] += jnp.where(earlier, second_unit, first_unit)
        sums[2] += jnp.where(earlier, 0, second_unit)
    near_sum = sums[0]
    ahead_sums = [value.astype(jnp.bfloat16) for value in sums[1:]]
    back = [
        passed_along(value, "img", hop * GROUP) for hop, value in enumerate(ahead_sums, start=1)
    ]

    near_late = near
    ahead = [
        near,
        passed_along(near_late, "img", -GROUP),
        passed_along(near_late, "img", -2 * GROUP),
    ]
    *ahead, _ = lax.optimization_barrier((*ahead, returns[0]))
    tables = [jnp.concatenate(ahead[1:])]
    for bits in range(1, GROUP):
        later = member > (member ^ bits)
        sent = jnp.where(later, jnp.concatenate(ahead[:2]), jnp.concatenate(ahead[1:]))
        tables.append(exchanged(sent, "img", bits))

    tables, near_sum, back = lax.optimization_barrier((tables, near_sum, back))
    own, send = pl.pallas_call(
        functools.partial(forward_kernel, per, devices),
        in_specs=[SMEM] * 3 + [VMEM] + [anywhere] + [VMEM] * GROUP,
        out_specs=[VMEM] * 2,
        out_shape=[jax.ShapeDtypeStruct((img_dev, half, univ), jnp.float32)] * 2,
        scratch_shapes=[
            pltpu.VMEM(blocks.shape, blocks.dtype),
            pltpu.VMEM((GROUP * units, cols, univ), jnp.bfloat16),
            pltpu.VMEM((img_dev + 1, keypts, univ), jnp.float32),
            pltpu.SemaphoreType.DMA((slots // per,)),
        ],
        compiler_params=LIMIT,
        cost_estimate=SHORT,
        name="forward",
    )(place, counts, pairs, panels, blocks, *tables)
    other_half = exchanged(send, "rep", 1)

    field, packed = pl.pallas_call(
        gram_kernel,
        in_specs=[VMEM] * 5,
        out_specs=[VMEM] * 2,
        out_shape=[
            jax.ShapeDtypeStruct(panels.shape, jnp.float32),
            jax.ShapeDtypeStruct((univ // 2 + ROWS, univ), jnp.float32),
        ],
        name="gram",
    )(own, other_half, near_sum, *back)
    terms = [packed, exchanged(packed, "rep", 1)]
    bits = 1
    while bits < devices:
        packed = sum(terms)
        terms = [packed] + [exchanged(packed, "img", bits * k) for k in range(1, min(4, devices // bits))]
        bits *= 4
    return pl.pallas_call(
        functools.partial(solve_kernel, 1 / (devices * img_dev * keypts), len(terms)),
        in_specs=[VMEM] * (len(terms) + 1),
        out_specs=VMEM,
        out_shape=jax.ShapeDtypeStruct(panels.shape, jnp.float32),
        scratch_shapes=[pltpu.VMEM((univ, univ), jnp.float32)],
        name="solve",
    )(*terms, field)


def solution(mesh):
    in_specs = (P("img", "rep", None), P("img", None, "rep"), P("img", None), P("img"))
    out_specs = P("img", "rep", None)
    return jax.shard_map(shards, mesh=mesh, in_specs=in_specs, out_specs=out_specs, check_vma=False)
```

```python
import functools

import jax
import jax.numpy as jnp
from jax import lax
from jax.experimental import pallas as pl
from jax.experimental.pallas import tpu as pltpu
from jax.sharding import PartitionSpec as P

BAND = 8
GROUP = BAND // 2
WAIT = 6
ROWS = 16
SMEM = pl.BlockSpec(memory_space=pltpu.SMEM)
VMEM = pl.BlockSpec(memory_space=pltpu.VMEM)
SHORT = pl.CostEstimate(flops=1, bytes_accessed=1, transcendentals=0)
LONG = pl.CostEstimate(flops=10**11, bytes_accessed=10**8, transcendentals=0)
SMALL = pltpu.CompilerParams(vmem_limit_bytes=8 << 20)
LIMIT = pltpu.CompilerParams(vmem_limit_bytes=50 << 20)


def passed_along(value, axis, steps):
    count = lax.axis_size(axis)
    pairs = [(source, (source + steps) % count) for source in range(count)]
    return lax.ppermute(value, axis, pairs)


def exchanged(value, axis, bits):
    count = lax.axis_size(axis)
    return lax.ppermute(value, axis, [(source, source ^ bits) for source in range(count)])


def entry(second, own_index, devices, img_dev):
    owner = lax.div(second, img_dev)
    member = lax.rem(owner, GROUP)
    own_member = lax.rem(own_index, GROUP)
    groups = devices // GROUP
    hop = lax.rem(lax.div(owner, GROUP) - lax.div(own_index, GROUP) + groups, groups)
    turn = hop - jnp.where(member <= own_member, 1, 0)
    return ((member ^ own_member) * 2 + turn) * img_dev + second - owner * img_dev


def start_kernel(panels, pairs, counts, near, numbers):
    near[...] = panels[...].astype(jnp.bfloat16)
    row = (1, pairs.shape[1])
    numbers[...] = jnp.zeros_like(numbers)
    numbers[pl.ds(0, 2), :] = pairs[...]
    numbers[pl.ds(2, 1), :] = jnp.broadcast_to(counts[...], row)
    numbers[pl.ds(3, 1), :] = jnp.full(row, lax.axis_index("rep"), jnp.int32)
    numbers[pl.ds(4, 1), :] = jnp.full(row, lax.axis_index("img"), jnp.int32)


def reverse_kernel(per, devices, numbers, near, far, blocks, *rest):
    outs, order, rest = rest[:GROUP], rest[GROUP : GROUP + 3], rest[GROUP + 3 :]
    kept, turned, total, landed, held, listed, filled = rest
    members, units_of, firsts = order
    bucket = members.shape[0] // GROUP
    slots = blocks.shape[0]
    img_dev, half = near.shape[0], near.shape[1]
    units = 2 * img_dev
    steps = slots // per

    def fetch(step):
        rows = pl.ds(step * per, per)
        return pltpu.make_async_copy(blocks.at[rows], kept.at[rows], landed.at[step])

    lists = pltpu.make_async_copy(numbers, held, listed)
    lists.start()
    for step in range(steps):
        fetch(step).start()
    for member in range(GROUP):
        filled[member] = 0
        for rank in range(bucket):
            members[member * bucket + rank] = 0
            units_of[member * bucket + rank] = 0
            firsts[member * bucket + rank] = img_dev
    lists.wait()
    count, core, own_index = held[2, 0], held[3, 0], held[4, 0]
    near_columns = pl.ds(pl.multiple_of(core * half, half), half)
    far_columns = pl.ds(pl.multiple_of((1 - core) * half, half), half)
    for image in range(img_dev):
        turned[image, :, near_columns] = near[image].T
        turned[image, :, far_columns] = far[image].T
    total[...] = jnp.zeros_like(total)

    @pl.loop(0, steps)
    def _(step):
        fetch(step).wait()
        for part in range(per):
            slot = step * per + part
            alive = slot < count
            place_in = entry(held[1, slot], own_index, devices, img_dev)
            first = held[0, slot] - own_index * img_dev
            apart = lax.div(place_in, units)
            rank = filled[apart]
            filled[apart] = rank + jnp.where(alive, 1, 0)
            members[apart * bucket + rank] = slot
            units_of[apart * bucket + rank] = place_in - apart * units
            firsts[apart * bucket + rank] = jnp.where(alive, first, img_dev)
            place_in = jnp.where(alive, place_in, GROUP * units)
            product = jnp.dot(turned[first], kept[slot], preferred_element_type=jnp.float32)
            total[place_in] += product.astype(jnp.bfloat16).astype(jnp.float32)

    for member in range(GROUP):
        for unit in range(units):
            outs[member][unit] = total[member * units + unit].astype(jnp.bfloat16).T


def forward_slots(picked, members, units, firsts, blocks, tables, kept, total, landed):
    bucket = members.shape[0] // GROUP
    listed = [member * bucket + rank for member in picked for rank in range(bucket)]

    def fetch(at):
        return pltpu.make_async_copy(blocks.at[members[listed[at]]], kept.at[at], landed.at[at])

    for at in range(len(listed)):
        fetch(at).start()
    for at, target in enumerate(listed):
        if at % WAIT == 0:
            for more in range(at, min(at + WAIT, len(listed))):
                fetch(more).wait()
        table = tables[at // bucket]
        total[firsts[target]] += jnp.dot(
            kept[at], table[units[target]], preferred_element_type=jnp.float32
        )


def forward_first_kernel(picked, members, units, firsts, blocks, *rest):
    tables, (sums, kept, total, landed) = rest[: len(picked)], rest[len(picked) :]
    total[...] = jnp.zeros_like(total)
    forward_slots(picked, members, units, firsts, blocks, tables, kept, total, landed)
    for image in range(sums.shape[0]):
        sums[image] = total[image]


def forward_last_kernel(picked, place, members, units, firsts, blocks, panels, before, *rest):
    tables, (own, send, kept, total, landed) = rest[: len(picked)], rest[len(picked) :]
    core = place[0]
    img_dev, half = panels.shape[0], panels.shape[1]
    total[...] = jnp.zeros_like(total)
    forward_slots(picked, members, units, firsts, blocks, tables, kept, total, landed)
    near_rows = pl.ds(pl.multiple_of(core * half, half), half)
    far_rows = pl.ds(pl.multiple_of((1 - core) * half, half), half)
    for image in range(img_dev):
        own[image] = panels[image] + before[image, near_rows] + total[image, near_rows]
        send[image] = before[image, far_rows] + total[image, far_rows]


def split(value):
    high = value.astype(jnp.bfloat16)
    return high, (value - high.astype(jnp.float32)).astype(jnp.bfloat16)


def gram_kernel(own, other, near_sum, back_one, back_two, field, packed):
    univ = packed.shape[1]
    gram = jnp.zeros((univ, 2 * univ), jnp.float32)
    for image in range(field.shape[0]):
        rows = own[image] + other[image] + near_sum[image]
        rows += back_one[image].astype(jnp.float32) + back_two[image].astype(jnp.float32)
        field[image] = rows
        high, low = split(rows)
        both = jnp.concatenate([high, low], axis=1)
        gram += lax.dot_general(
            high, both, (((0,), (0,)), ((), ())), preferred_element_type=jnp.float32
        )
    crossed = gram[:, univ:]
    gram = gram[:, :univ] + crossed + crossed.T
    side = univ // 2
    row_ids = lax.broadcasted_iota(jnp.int32, (side, side), 0)
    column_ids = lax.broadcasted_iota(jnp.int32, (side, side), 1)
    last = gram[side:, side:]
    mixed = jnp.where(row_ids <= column_ids, gram[:side, :side], last)
    packed[pl.ds(0, side), :] = jnp.concatenate([mixed, gram[:side, side:]], axis=1)
    diagonal = jnp.sum(jnp.where(row_ids == column_ids, last, 0.0), axis=0, keepdims=True)
    diagonal = jnp.concatenate([diagonal, diagonal], axis=1)
    packed[pl.ds(side, 8), :] = jnp.broadcast_to(diagonal, (8, univ))


def solve_kernel(scale, terms, *rest):
    packs, (field, basis, inverse) = rest[:terms], rest[terms:]
    univ = inverse.shape[0]
    side = univ // 2
    packed = packs[0][...]
    for pack in packs[1:]:
        packed += pack[...]
    packed *= scale
    row_ids = lax.broadcasted_iota(jnp.int32, (side, side), 0)
    column_ids = lax.broadcasted_iota(jnp.int32, (side, side), 1)
    mixed = packed[:side, :side]
    turned = mixed.T
    head = jnp.where(row_ids <= column_ids, mixed, turned)
    last = jnp.where(row_ids > column_ids, mixed, turned)
    diagonal = jnp.broadcast_to(packed[side : side + 1, :side], (side, side))
    last = jnp.where(row_ids == column_ids, diagonal, last)
    inverse[pl.ds(0, side), :] = jnp.concatenate([head, packed[:side, side:]], axis=1)
    inverse[pl.ds(side, side), :] = jnp.concatenate([last, last], axis=1)

    count = univ // ROWS
    shape = (ROWS, univ)
    row_ids = lax.broadcasted_iota(jnp.int32, shape, 0)
    column_ids = lax.broadcasted_iota(jnp.int32, shape, 1)
    left = [inverse[pl.ds(b * ROWS, ROWS), :] for b in range(count)]
    right = [
        jnp.where(column_ids == row_ids + b * ROWS, 1.0, 0.0).astype(jnp.float32)
        for b in range(count)
    ]

    def spread(value, row):
        return jnp.broadcast_to(value[row : row + 1, :], shape)

    for b in range(count):
        rows, tail = left[b], right[b]
        columns = [
            jnp.broadcast_to(rows[:, b * ROWS + j : b * ROWS + j + 1], shape) for j in range(ROWS)
        ]
        pivots = jnp.ones(shape, jnp.float32)
        for j in range(ROWS):
            pivot = spread(columns[j], j)
            pivots = jnp.where(row_ids == j, pivot, pivots)
            if j < ROWS - 1:
                weight = jnp.where(row_ids > j, columns[j] * (1.0 / pivot), 0.0)
                for k in range(j + 1, ROWS):
                    columns[k] = columns[k] - weight * spread(columns[k], j)
                rows = rows - weight * spread(rows, j)
                tail = tail - weight * spread(tail, j)
        inverse[pl.ds(b * ROWS, ROWS), :] = tail * lax.rsqrt(pivots)
        if b < count - 1:
            turned = (rows * (1.0 / pivots)).T
            for c in range(b + 1, count):
                for j in range(ROWS):
                    weight = jnp.broadcast_to(turned[c * ROWS : (c + 1) * ROWS, j : j + 1], shape)
                    left[c] = left[c] - weight * spread(rows, j)
                    right[c] = right[c] - weight * spread(tail, j)
    inverse_high, inverse_low = split(inverse[...].T)
    wide = jnp.concatenate([inverse_high, inverse_low], axis=1)
    for image in range(field.shape[0]):
        high, low = split(field[image])
        products = jnp.dot(high, wide, preferred_element_type=jnp.float32)
        products = products[:, :univ] + products[:, univ:]
        basis[image] = products + jnp.dot(
            low, inverse_high, preferred_element_type=jnp.float32
        )


def shards(panels, blocks, pairs, counts):
    devices = lax.axis_size("img")
    own_index = lax.axis_index("img")
    member = own_index % GROUP
    img_dev, half, univ = panels.shape
    slots, keypts, cols = blocks.shape
    units = 2 * img_dev
    per = next(width for width in (8, 6, 4, 3, 2, 1) if slots % width == 0)
    place = jnp.stack([lax.axis_index("rep"), own_index]).astype(jnp.int32)
    anywhere = pl.BlockSpec(memory_space=pl.ANY)

    near, numbers = pl.pallas_call(
        start_kernel,
        in_specs=[VMEM] * 3,
        out_specs=[VMEM] * 2,
        out_shape=[
            jax.ShapeDtypeStruct(panels.shape, jnp.bfloat16),
            jax.ShapeDtypeStruct((8, slots), jnp.int32),
        ],
        compiler_params=SMALL,
        name="start",
    )(panels, pairs.T, counts.reshape(1, 1))
    far = exchanged(near, "rep", 1)
    bucket = 2 * (slots // BAND)
    *returns, members, units_of, firsts = pl.pallas_call(
        functools.partial(reverse_kernel, per, devices),
        in_specs=[anywhere] + [VMEM] * 2 + [anywhere],
        out_specs=[VMEM] * GROUP + [SMEM] * 3,
        out_shape=[jax.ShapeDtypeStruct((units, cols, univ), jnp.bfloat16)] * GROUP
        + [jax.ShapeDtypeStruct((GROUP * bucket,), jnp.int32)] * 3,
        scratch_shapes=[
            pltpu.VMEM(blocks.shape, blocks.dtype),
            pltpu.VMEM((img_dev, univ, keypts), jnp.bfloat16),
            pltpu.VMEM((GROUP * units + 1, univ, cols), jnp.float32),
            pltpu.SemaphoreType.DMA((slots // per,)),
            pltpu.SMEM(numbers.shape, numbers.dtype),
            pltpu.SemaphoreType.DMA(()),
            pltpu.SMEM((GROUP,), jnp.int32),
        ],
        compiler_params=LIMIT,
        cost_estimate=SHORT,
        name="reverse",
    )(numbers, near, far, blocks)

    arrived = [exchanged(returns[bits], "img", bits) for bits in range(1, GROUP)]
    part = (img_dev, cols, univ)
    sums = [jnp.zeros(part, jnp.float32) for _ in range(3)]
    for bits, value in enumerate([returns[0]] + arrived):
        first_unit = value[:img_dev].astype(jnp.float32)
        second_unit = value[img_dev:].astype(jnp.float32)
        earlier = (member ^ bits) < member
        sums[0] += jnp.where(earlier, first_unit, 0)
        sums[1] += jnp.where(earlier, second_unit, first_unit)
        sums[2] += jnp.where(earlier, 0, second_unit)
    near_sum = sums[0]
    ahead_sums = [value.astype(jnp.bfloat16) for value in sums[1:]]
    back = [
        passed_along(value, "img", hop * GROUP) for hop, value in enumerate(ahead_sums, start=1)
    ]

    near_late = near
    ahead = [
        near,
        passed_along(near_late, "img", -GROUP),
        passed_along(near_late, "img", -2 * GROUP),
    ]
    *ahead, _ = lax.optimization_barrier((*ahead, returns[0]))
    tables = [jnp.concatenate(ahead[1:])]
    for bits in range(1, GROUP):
        later = member > (member ^ bits)
        sent = jnp.where(later, jnp.concatenate(ahead[:2]), jnp.concatenate(ahead[1:]))
        tables.append(exchanged(sent, "img", bits))

    def forward_scratch(picked):
        return [
            pltpu.VMEM((len(picked) * bucket, keypts, cols), jnp.bfloat16),
            pltpu.VMEM((img_dev + 1, keypts, univ), jnp.float32),
            pltpu.SemaphoreType.DMA((len(picked) * bucket,)),
        ]

    early, late = tuple(range(GROUP // 2)), tuple(range(GROUP // 2, GROUP))
    members, units_of, firsts, _ = lax.optimization_barrier((members, units_of, firsts, near_sum))
    before = pl.pallas_call(
        functools.partial(forward_first_kernel, early),
        in_specs=[SMEM] * 3 + [anywhere] + [VMEM] * len(early),
        out_specs=VMEM,
        out_shape=jax.ShapeDtypeStruct((img_dev, keypts, univ), jnp.float32),
        scratch_shapes=forward_scratch(early),
        compiler_params=LIMIT,
        cost_estimate=SHORT,
        name="forward_first",
    )(members, units_of, firsts, blocks, *[tables[index] for index in early])
    last_tables = [tables[index] for index in late]
    last_tables, near_sum, back = lax.optimization_barrier((last_tables, near_sum, back))
    own, send = pl.pallas_call(
        functools.partial(forward_last_kernel, late),
        in_specs=[SMEM] * 4 + [anywhere] + [VMEM] * (2 + len(late)),
        out_specs=[VMEM] * 2,
        out_shape=[jax.ShapeDtypeStruct((img_dev, half, univ), jnp.float32)] * 2,
        scratch_shapes=forward_scratch(late),
        compiler_params=LIMIT,
        cost_estimate=SHORT,
        name="forward_last",
    )(place, members, units_of, firsts, blocks, panels, before, *last_tables)
    other_half = exchanged(send, "rep", 1)

    field, packed = pl.pallas_call(
        gram_kernel,
        in_specs=[VMEM] * 5,
        out_specs=[VMEM] * 2,
        out_shape=[
            jax.ShapeDtypeStruct(panels.shape, jnp.float32),
            jax.ShapeDtypeStruct((univ // 2 + 8, univ), jnp.float32),
        ],
        compiler_params=SMALL,
        name="gram",
    )(own, other_half, near_sum, *back)
    terms = [packed, exchanged(packed, "rep", 1)]
    bits = 1
    while bits < devices:
        packed = sum(terms)
        terms = [packed] + [exchanged(packed, "img", bits * k) for k in range(1, min(4, devices // bits))]
        bits *= 4
    return pl.pallas_call(
        functools.partial(solve_kernel, 1 / (devices * img_dev * keypts), len(terms)),
        in_specs=[VMEM] * (len(terms) + 1),
        out_specs=VMEM,
        out_shape=jax.ShapeDtypeStruct(panels.shape, jnp.float32),
        scratch_shapes=[pltpu.VMEM((univ, univ), jnp.float32)],
        compiler_params=SMALL,
        name="solve",
    )(*terms, field)


def solution(mesh):
    in_specs = (P("img", "rep", None), P("img", None, "rep"), P("img", None), P("img"))
    out_specs = P("img", "rep", None)
    return jax.shard_map(shards, mesh=mesh, in_specs=in_specs, out_specs=out_specs, check_vma=False)
```

```python
import functools

import jax
import jax.numpy as jnp
from jax import lax
from jax.experimental import pallas as pl
from jax.experimental.pallas import tpu as pltpu
from jax.sharding import PartitionSpec as P

BAND = 8
GROUP = BAND // 2
WAIT = 6
ROWS = 16
SMEM = pl.BlockSpec(memory_space=pltpu.SMEM)
VMEM = pl.BlockSpec(memory_space=pltpu.VMEM)
SHORT = pl.CostEstimate(flops=1, bytes_accessed=1, transcendentals=0)
LONG = pl.CostEstimate(flops=10**11, bytes_accessed=10**8, transcendentals=0)
SMALL = pltpu.CompilerParams(vmem_limit_bytes=8 << 20)
LIMIT = pltpu.CompilerParams(vmem_limit_bytes=50 << 20)


def passed_along(value, axis, steps):
    count = lax.axis_size(axis)
    pairs = [(source, (source + steps) % count) for source in range(count)]
    return lax.ppermute(value, axis, pairs)


def exchanged(value, axis, bits):
    count = lax.axis_size(axis)
    return lax.ppermute(value, axis, [(source, source ^ bits) for source in range(count)])


def entry(second, own_index, devices, img_dev):
    owner = lax.div(second, img_dev)
    member = lax.rem(owner, GROUP)
    own_member = lax.rem(own_index, GROUP)
    groups = devices // GROUP
    hop = lax.rem(lax.div(owner, GROUP) - lax.div(own_index, GROUP) + groups, groups)
    turn = hop - jnp.where(member <= own_member, 1, 0)
    return ((member ^ own_member) * 2 + turn) * img_dev + second - owner * img_dev


def start_kernel(panels, pairs, counts, near, numbers):
    near[...] = panels[...].astype(jnp.bfloat16)
    row = (1, pairs.shape[1])
    numbers[...] = jnp.zeros_like(numbers)
    numbers[pl.ds(0, 2), :] = pairs[...]
    numbers[pl.ds(2, 1), :] = jnp.broadcast_to(counts[...], row)
    numbers[pl.ds(3, 1), :] = jnp.full(row, lax.axis_index("rep"), jnp.int32)
    numbers[pl.ds(4, 1), :] = jnp.full(row, lax.axis_index("img"), jnp.int32)


def reverse_kernel(per, devices, numbers, near, far, blocks, *rest):
    outs, order, rest = rest[:GROUP], rest[GROUP : GROUP + 3], rest[GROUP + 3 :]
    kept, turned, total, landed, held, listed, filled = rest
    members, units_of, firsts = order
    bucket = members.shape[0] // GROUP
    slots = blocks.shape[0]
    img_dev, half = near.shape[0], near.shape[1]
    units = 2 * img_dev
    steps = slots // per

    def fetch(step):
        rows = pl.ds(step * per, per)
        return pltpu.make_async_copy(blocks.at[rows], kept.at[rows], landed.at[step])

    lists = pltpu.make_async_copy(numbers, held, listed)
    lists.start()
    for step in range(steps):
        fetch(step).start()
    for member in range(GROUP):
        filled[member] = 0
        for rank in range(bucket):
            members[member * bucket + rank] = 0
            units_of[member * bucket + rank] = 0
            firsts[member * bucket + rank] = img_dev
    lists.wait()
    count, core, own_index = held[2, 0], held[3, 0], held[4, 0]
    near_columns = pl.ds(pl.multiple_of(core * half, half), half)
    far_columns = pl.ds(pl.multiple_of((1 - core) * half, half), half)
    for image in range(img_dev):
        turned[image, :, near_columns] = near[image].T
        turned[image, :, far_columns] = far[image].T
    total[...] = jnp.zeros_like(total)

    @pl.loop(0, steps)
    def _(step):
        fetch(step).wait()
        for part in range(per):
            slot = step * per + part
            alive = slot < count
            place_in = entry(held[1, slot], own_index, devices, img_dev)
            first = held[0, slot] - own_index * img_dev
            apart = lax.div(place_in, units)
            rank = filled[apart]
            filled[apart] = rank + jnp.where(alive, 1, 0)
            members[apart * bucket + rank] = slot
            units_of[apart * bucket + rank] = place_in - apart * units
            firsts[apart * bucket + rank] = jnp.where(alive, first, img_dev)
            place_in = jnp.where(alive, place_in, GROUP * units)
            product = jnp.dot(turned[first], kept[slot], preferred_element_type=jnp.float32)
            total[place_in] += product.astype(jnp.bfloat16).astype(jnp.float32)

    for member in range(GROUP):
        for unit in range(units):
            outs[member][unit] = total[member * units + unit].astype(jnp.bfloat16).T


def forward_slots(picked, members, units, firsts, blocks, tables, kept, total, landed):
    bucket = members.shape[0] // GROUP
    listed = [member * bucket + rank for member in picked for rank in range(bucket)]

    def fetch(at):
        return pltpu.make_async_copy(blocks.at[members[listed[at]]], kept.at[at], landed.at[at])

    for at in range(len(listed)):
        fetch(at).start()
    total[...] = jnp.zeros_like(total)
    for at, target in enumerate(listed):
        if at % WAIT == 0:
            for more in range(at, min(at + WAIT, len(listed))):
                fetch(more).wait()
        table = tables[at // bucket]
        total[firsts[target]] += jnp.dot(
            kept[at], table[units[target]], preferred_element_type=jnp.float32
        )


def forward_first_kernel(picked, members, units, firsts, blocks, *rest):
    tables, (sums, kept, total, landed) = rest[: len(picked)], rest[len(picked) :]
    forward_slots(picked, members, units, firsts, blocks, tables, kept, total, landed)
    for image in range(sums.shape[0]):
        sums[image] = total[image]


def forward_next_kernel(picked, members, units, firsts, blocks, before, *rest):
    tables, (sums, kept, total, landed) = rest[: len(picked)], rest[len(picked) :]
    forward_slots(picked, members, units, firsts, blocks, tables, kept, total, landed)
    for image in range(sums.shape[0]):
        sums[image] = before[image] + total[image]


def forward_last_kernel(picked, place, members, units, firsts, blocks, panels, before, *rest):
    tables, (own, send, kept, total, landed) = rest[: len(picked)], rest[len(picked) :]
    core = place[0]
    img_dev, half = panels.shape[0], panels.shape[1]
    forward_slots(picked, members, units, firsts, blocks, tables, kept, total, landed)
    near_rows = pl.ds(pl.multiple_of(core * half, half), half)
    far_rows = pl.ds(pl.multiple_of((1 - core) * half, half), half)
    for image in range(img_dev):
        own[image] = panels[image] + before[image, near_rows] + total[image, near_rows]
        send[image] = before[image, far_rows] + total[image, far_rows]


def split(value):
    high = value.astype(jnp.bfloat16)
    return high, (value - high.astype(jnp.float32)).astype(jnp.bfloat16)


def gram_kernel(own, other, near_sum, back_one, back_two, field, packed):
    univ = packed.shape[1]
    gram = jnp.zeros((univ, 2 * univ), jnp.float32)
    for image in range(field.shape[0]):
        rows = own[image] + other[image] + near_sum[image]
        rows += back_one[image].astype(jnp.float32) + back_two[image].astype(jnp.float32)
        field[image] = rows
        high, low = split(rows)
        both = jnp.concatenate([high, low], axis=1)
        gram += lax.dot_general(
            high, both, (((0,), (0,)), ((), ())), preferred_element_type=jnp.float32
        )
    crossed = gram[:, univ:]
    gram = gram[:, :univ] + crossed + crossed.T
    side = univ // 2
    row_ids = lax.broadcasted_iota(jnp.int32, (side, side), 0)
    column_ids = lax.broadcasted_iota(jnp.int32, (side, side), 1)
    last = gram[side:, side:]
    mixed = jnp.where(row_ids <= column_ids, gram[:side, :side], last)
    packed[pl.ds(0, side), :] = jnp.concatenate([mixed, gram[:side, side:]], axis=1)
    diagonal = jnp.sum(jnp.where(row_ids == column_ids, last, 0.0), axis=0, keepdims=True)
    diagonal = jnp.concatenate([diagonal, diagonal], axis=1)
    packed[pl.ds(side, 8), :] = jnp.broadcast_to(diagonal, (8, univ))


def solve_kernel(scale, terms, *rest):
    packs, (field, basis, inverse) = rest[:terms], rest[terms:]
    univ = inverse.shape[0]
    side = univ // 2
    packed = packs[0][...]
    for pack in packs[1:]:
        packed += pack[...]
    packed *= scale
    row_ids = lax.broadcasted_iota(jnp.int32, (side, side), 0)
    column_ids = lax.broadcasted_iota(jnp.int32, (side, side), 1)
    mixed = packed[:side, :side]
    turned = mixed.T
    head = jnp.where(row_ids <= column_ids, mixed, turned)
    last = jnp.where(row_ids > column_ids, mixed, turned)
    diagonal = jnp.broadcast_to(packed[side : side + 1, :side], (side, side))
    last = jnp.where(row_ids == column_ids, diagonal, last)
    inverse[pl.ds(0, side), :] = jnp.concatenate([head, packed[:side, side:]], axis=1)
    inverse[pl.ds(side, side), :] = jnp.concatenate([last, last], axis=1)

    count = univ // ROWS
    shape = (ROWS, univ)
    row_ids = lax.broadcasted_iota(jnp.int32, shape, 0)
    column_ids = lax.broadcasted_iota(jnp.int32, shape, 1)
    left = [inverse[pl.ds(b * ROWS, ROWS), :] for b in range(count)]
    right = [
        jnp.where(column_ids == row_ids + b * ROWS, 1.0, 0.0).astype(jnp.float32)
        for b in range(count)
    ]

    def spread(value, row):
        return jnp.broadcast_to(value[row : row + 1, :], shape)

    for b in range(count):
        rows, tail = left[b], right[b]
        columns = [
            jnp.broadcast_to(rows[:, b * ROWS + j : b * ROWS + j + 1], shape) for j in range(ROWS)
        ]
        pivots = jnp.ones(shape, jnp.float32)
        for j in range(ROWS):
            pivot = spread(columns[j], j)
            pivots = jnp.where(row_ids == j, pivot, pivots)
            if j < ROWS - 1:
                weight = jnp.where(row_ids > j, columns[j] * (1.0 / pivot), 0.0)
                for k in range(j + 1, ROWS):
                    columns[k] = columns[k] - weight * spread(columns[k], j)
                rows = rows - weight * spread(rows, j)
                tail = tail - weight * spread(tail, j)
        inverse[pl.ds(b * ROWS, ROWS), :] = tail * lax.rsqrt(pivots)
        if b < count - 1:
            turned = (rows * (1.0 / pivots)).T
            for c in range(b + 1, count):
                for j in range(ROWS):
                    weight = jnp.broadcast_to(turned[c * ROWS : (c + 1) * ROWS, j : j + 1], shape)
                    left[c] = left[c] - weight * spread(rows, j)
                    right[c] = right[c] - weight * spread(tail, j)
    inverse_high, inverse_low = split(inverse[...].T)
    wide = jnp.concatenate([inverse_high, inverse_low], axis=1)
    for image in range(field.shape[0]):
        high, low = split(field[image])
        products = jnp.dot(high, wide, preferred_element_type=jnp.float32)
        products = products[:, :univ] + products[:, univ:]
        basis[image] = products + jnp.dot(
            low, inverse_high, preferred_element_type=jnp.float32
        )


def shards(panels, blocks, pairs, counts):
    devices = lax.axis_size("img")
    own_index = lax.axis_index("img")
    member = own_index % GROUP
    img_dev, half, univ = panels.shape
    slots, keypts, cols = blocks.shape
    units = 2 * img_dev
    per = next(width for width in (8, 6, 4, 3, 2, 1) if slots % width == 0)
    place = jnp.stack([lax.axis_index("rep"), own_index]).astype(jnp.int32)
    anywhere = pl.BlockSpec(memory_space=pl.ANY)

    near, numbers = pl.pallas_call(
        start_kernel,
        in_specs=[VMEM] * 3,
        out_specs=[VMEM] * 2,
        out_shape=[
            jax.ShapeDtypeStruct(panels.shape, jnp.bfloat16),
            jax.ShapeDtypeStruct((8, slots), jnp.int32),
        ],
        compiler_params=SMALL,
        name="start",
    )(panels, pairs.T, counts.reshape(1, 1))
    far = exchanged(near, "rep", 1)
    bucket = 2 * (slots // BAND)
    *returns, members, units_of, firsts = pl.pallas_call(
        functools.partial(reverse_kernel, per, devices),
        in_specs=[anywhere] + [VMEM] * 2 + [anywhere],
        out_specs=[VMEM] * GROUP + [SMEM] * 3,
        out_shape=[jax.ShapeDtypeStruct((units, cols, univ), jnp.bfloat16)] * GROUP
        + [jax.ShapeDtypeStruct((GROUP * bucket,), jnp.int32)] * 3,
        scratch_shapes=[
            pltpu.VMEM(blocks.shape, blocks.dtype),
            pltpu.VMEM((img_dev, univ, keypts), jnp.bfloat16),
            pltpu.VMEM((GROUP * units + 1, univ, cols), jnp.float32),
            pltpu.SemaphoreType.DMA((slots // per,)),
            pltpu.SMEM(numbers.shape, numbers.dtype),
            pltpu.SemaphoreType.DMA(()),
            pltpu.SMEM((GROUP,), jnp.int32),
        ],
        compiler_params=LIMIT,
        cost_estimate=SHORT,
        name="reverse",
    )(numbers, near, far, blocks)

    arrived = [exchanged(returns[bits], "img", bits) for bits in range(1, GROUP)]
    part = (img_dev, cols, univ)
    sums = [jnp.zeros(part, jnp.float32) for _ in range(3)]
    for bits, value in enumerate([returns[0]] + arrived):
        first_unit = value[:img_dev].astype(jnp.float32)
        second_unit = value[img_dev:].astype(jnp.float32)
        earlier = (member ^ bits) < member
        sums[0] += jnp.where(earlier, first_unit, 0)
        sums[1] += jnp.where(earlier, second_unit, first_unit)
        sums[2] += jnp.where(earlier, 0, second_unit)
    near_sum = sums[0]
    ahead_sums = [value.astype(jnp.bfloat16) for value in sums[1:]]
    back = [
        passed_along(value, "img", hop * GROUP) for hop, value in enumerate(ahead_sums, start=1)
    ]

    near_late = near
    ahead = [
        near,
        passed_along(near_late, "img", -GROUP),
        passed_along(near_late, "img", -2 * GROUP),
    ]
    *ahead, _ = lax.optimization_barrier((*ahead, returns[0]))
    tables = [jnp.concatenate(ahead[1:])]
    def forward_scratch(picked):
        return [
            pltpu.VMEM((len(picked) * bucket, keypts, cols), jnp.bfloat16),
            pltpu.VMEM((img_dev + 1, keypts, univ), jnp.float32),
            pltpu.SemaphoreType.DMA((len(picked) * bucket,)),
        ]

    before = pl.pallas_call(
        functools.partial(forward_first_kernel, (0,)),
        in_specs=[SMEM] * 3 + [anywhere, VMEM],
        out_specs=VMEM,
        out_shape=jax.ShapeDtypeStruct((img_dev, keypts, univ), jnp.float32),
        scratch_shapes=forward_scratch((0,)),
        compiler_params=LIMIT,
        cost_estimate=SHORT,
        name="forward_first",
    )(members, units_of, firsts, blocks, tables[0])
    for bits in range(1, GROUP):
        later = member > (member ^ bits)
        if bits == GROUP - 1:
            *ahead, before, arrived[1] = lax.optimization_barrier((*ahead, before, arrived[1]))
        sent = jnp.where(later, jnp.concatenate(ahead[:2]), jnp.concatenate(ahead[1:]))
        tables.append(exchanged(sent, "img", bits))

    middle, late = tuple(range(1, GROUP - 1)), (GROUP - 1,)
    before = pl.pallas_call(
        functools.partial(forward_next_kernel, middle),
        in_specs=[SMEM] * 3 + [anywhere] + [VMEM] * (1 + len(middle)),
        out_specs=VMEM,
        out_shape=jax.ShapeDtypeStruct((img_dev, keypts, univ), jnp.float32),
        scratch_shapes=forward_scratch(middle),
        compiler_params=LIMIT,
        cost_estimate=SHORT,
        name="forward_next",
    )(members, units_of, firsts, blocks, before, *[tables[index] for index in middle])
    last_tables = [tables[index] for index in late]
    last_tables, near_sum, back = lax.optimization_barrier((last_tables, near_sum, back))
    own, send = pl.pallas_call(
        functools.partial(forward_last_kernel, late),
        in_specs=[SMEM] * 4 + [anywhere] + [VMEM] * (2 + len(late)),
        out_specs=[VMEM] * 2,
        out_shape=[jax.ShapeDtypeStruct((img_dev, half, univ), jnp.float32)] * 2,
        scratch_shapes=forward_scratch(late),
        compiler_params=LIMIT,
        cost_estimate=SHORT,
        name="forward_last",
    )(place, members, units_of, firsts, blocks, panels, before, *last_tables)
    other_half = exchanged(send, "rep", 1)

    field, packed = pl.pallas_call(
        gram_kernel,
        in_specs=[VMEM] * 5,
        out_specs=[VMEM] * 2,
        out_shape=[
            jax.ShapeDtypeStruct(panels.shape, jnp.float32),
            jax.ShapeDtypeStruct((univ // 2 + 8, univ), jnp.float32),
        ],
        compiler_params=SMALL,
        name="gram",
    )(own, other_half, near_sum, *back)
    terms = [packed, exchanged(packed, "rep", 1)]
    bits = 1
    while bits < devices:
        packed = sum(terms)
        terms = [packed] + [exchanged(packed, "img", bits * k) for k in range(1, min(4, devices // bits))]
        bits *= 4
    return pl.pallas_call(
        functools.partial(solve_kernel, 1 / (devices * img_dev * keypts), len(terms)),
        in_specs=[VMEM] * (len(terms) + 1),
        out_specs=VMEM,
        out_shape=jax.ShapeDtypeStruct(panels.shape, jnp.float32),
        scratch_shapes=[pltpu.VMEM((univ, univ), jnp.float32)],
        compiler_params=SMALL,
        name="solve",
    )(*terms, field)


def solution(mesh):
    in_specs = (P("img", "rep", None), P("img", None, "rep"), P("img", None), P("img"))
    out_specs = P("img", "rep", None)
    return jax.shard_map(shards, mesh=mesh, in_specs=in_specs, out_specs=out_specs, check_vma=False)
```

```python
import functools

import jax
import jax.numpy as jnp
from jax import lax
from jax.experimental import pallas as pl
from jax.experimental.pallas import tpu as pltpu
from jax.sharding import PartitionSpec as P

BAND = 8
GROUP = BAND // 2
WAIT = 6
ROWS = 16
SMEM = pl.BlockSpec(memory_space=pltpu.SMEM)
VMEM = pl.BlockSpec(memory_space=pltpu.VMEM)
SHORT = pl.CostEstimate(flops=1, bytes_accessed=1, transcendentals=0)
LONG = pl.CostEstimate(flops=10**11, bytes_accessed=10**8, transcendentals=0)
SMALL = pltpu.CompilerParams(vmem_limit_bytes=8 << 20)
LIMIT = pltpu.CompilerParams(vmem_limit_bytes=50 << 20)


def passed_along(value, axis, steps):
    count = lax.axis_size(axis)
    pairs = [(source, (source + steps) % count) for source in range(count)]
    return lax.ppermute(value, axis, pairs)


def exchanged(value, axis, bits):
    count = lax.axis_size(axis)
    return lax.ppermute(value, axis, [(source, source ^ bits) for source in range(count)])


def entry(second, own_index, devices, img_dev):
    owner = lax.div(second, img_dev)
    member = lax.rem(owner, GROUP)
    own_member = lax.rem(own_index, GROUP)
    groups = devices // GROUP
    hop = lax.rem(lax.div(owner, GROUP) - lax.div(own_index, GROUP) + groups, groups)
    turn = hop - jnp.where(member <= own_member, 1, 0)
    return ((member ^ own_member) * 2 + turn) * img_dev + second - owner * img_dev


def start_kernel(panels, pairs, counts, near, numbers):
    near[...] = panels[...].astype(jnp.bfloat16)
    row = (1, pairs.shape[1])
    numbers[...] = jnp.zeros_like(numbers)
    numbers[pl.ds(0, 2), :] = pairs[...]
    numbers[pl.ds(2, 1), :] = jnp.broadcast_to(counts[...], row)
    numbers[pl.ds(3, 1), :] = jnp.full(row, lax.axis_index("rep"), jnp.int32)
    numbers[pl.ds(4, 1), :] = jnp.full(row, lax.axis_index("img"), jnp.int32)


def reverse_kernel(per, devices, numbers, near, far, blocks, *rest):
    outs, order, rest = rest[:GROUP], rest[GROUP : GROUP + 3], rest[GROUP + 3 :]
    kept, turned, total, landed, held, listed, filled = rest
    members, units_of, firsts = order
    bucket = members.shape[0] // GROUP
    slots = blocks.shape[0]
    img_dev, half = near.shape[0], near.shape[1]
    units = 2 * img_dev
    steps = slots // per

    def fetch(step):
        rows = pl.ds(step * per, per)
        return pltpu.make_async_copy(blocks.at[rows], kept.at[rows], landed.at[step])

    lists = pltpu.make_async_copy(numbers, held, listed)
    lists.start()
    for step in range(steps):
        fetch(step).start()
    for member in range(GROUP):
        filled[member] = 0
        for rank in range(bucket):
            members[member * bucket + rank] = 0
            units_of[member * bucket + rank] = 0
            firsts[member * bucket + rank] = img_dev
    lists.wait()
    count, core, own_index = held[2, 0], held[3, 0], held[4, 0]
    near_columns = pl.ds(pl.multiple_of(core * half, half), half)
    far_columns = pl.ds(pl.multiple_of((1 - core) * half, half), half)
    for image in range(img_dev):
        turned[image, :, near_columns] = near[image].T
        turned[image, :, far_columns] = far[image].T
    total[...] = jnp.zeros_like(total)

    @pl.loop(0, steps)
    def _(step):
        fetch(step).wait()
        for part in range(per):
            slot = step * per + part
            alive = slot < count
            place_in = entry(held[1, slot], own_index, devices, img_dev)
            first = held[0, slot] - own_index * img_dev
            apart = lax.div(place_in, units)
            rank = filled[apart]
            filled[apart] = rank + jnp.where(alive, 1, 0)
            target = jnp.where(alive, apart * bucket + rank, GROUP * bucket)
            members[target] = slot
            units_of[target] = place_in - apart * units
            firsts[target] = first
            place_in = jnp.where(alive, place_in, GROUP * units)
            product = jnp.dot(turned[first], kept[slot], preferred_element_type=jnp.float32)
            total[place_in] += product.astype(jnp.bfloat16).astype(jnp.float32)

    for member in range(GROUP):
        for unit in range(units):
            outs[member][unit] = total[member * units + unit].astype(jnp.bfloat16).T


def forward_slots(picked, members, units, firsts, blocks, tables, kept, total, landed):
    bucket = members.shape[0] // GROUP
    listed = [member * bucket + rank for member in picked for rank in range(bucket)]

    def fetch(at):
        return pltpu.make_async_copy(blocks.at[members[listed[at]]], kept.at[at], landed.at[at])

    for at in range(len(listed)):
        fetch(at).start()
    total[...] = jnp.zeros_like(total)
    for at, target in enumerate(listed):
        if at % WAIT == 0:
            for more in range(at, min(at + WAIT, len(listed))):
                fetch(more).wait()
        table = tables[at // bucket]
        total[firsts[target]] += jnp.dot(
            kept[at], table[units[target]], preferred_element_type=jnp.float32
        )


def forward_first_kernel(picked, members, units, firsts, blocks, *rest):
    tables, (sums, kept, total, landed) = rest[: len(picked)], rest[len(picked) :]
    forward_slots(picked, members, units, firsts, blocks, tables, kept, total, landed)
    for image in range(sums.shape[0]):
        sums[image] = total[image]


def forward_next_kernel(picked, members, units, firsts, blocks, before, *rest):
    tables, (sums, kept, total, landed) = rest[: len(picked)], rest[len(picked) :]
    forward_slots(picked, members, units, firsts, blocks, tables, kept, total, landed)
    for image in range(sums.shape[0]):
        sums[image] = before[image] + total[image]


def forward_last_kernel(picked, place, members, units, firsts, blocks, panels, before, *rest):
    tables, (own, send, kept, total, landed) = rest[: len(picked)], rest[len(picked) :]
    core = place[0]
    img_dev, half = panels.shape[0], panels.shape[1]
    forward_slots(picked, members, units, firsts, blocks, tables, kept, total, landed)
    near_rows = pl.ds(pl.multiple_of(core * half, half), half)
    far_rows = pl.ds(pl.multiple_of((1 - core) * half, half), half)
    for image in range(img_dev):
        own[image] = panels[image] + before[image, near_rows] + total[image, near_rows]
        send[image] = before[image, far_rows] + total[image, far_rows]


def split(value):
    high = value.astype(jnp.bfloat16)
    return high, (value - high.astype(jnp.float32)).astype(jnp.bfloat16)


def gram_kernel(own, other, near_sum, back_one, back_two, field, packed):
    univ = packed.shape[1]
    gram = jnp.zeros((univ, 2 * univ), jnp.float32)
    for image in range(field.shape[0]):
        rows = own[image] + other[image] + near_sum[image]
        rows += back_one[image].astype(jnp.float32) + back_two[image].astype(jnp.float32)
        field[image] = rows
        high, low = split(rows)
        both = jnp.concatenate([high, low], axis=1)
        gram += lax.dot_general(
            high, both, (((0,), (0,)), ((), ())), preferred_element_type=jnp.float32
        )
    crossed = gram[:, univ:]
    gram = gram[:, :univ] + crossed + crossed.T
    side = univ // 2
    row_ids = lax.broadcasted_iota(jnp.int32, (side, side), 0)
    column_ids = lax.broadcasted_iota(jnp.int32, (side, side), 1)
    last = gram[side:, side:]
    mixed = jnp.where(row_ids <= column_ids, gram[:side, :side], last)
    packed[pl.ds(0, side), :] = jnp.concatenate([mixed, gram[:side, side:]], axis=1)
    diagonal = jnp.sum(jnp.where(row_ids == column_ids, last, 0.0), axis=0, keepdims=True)
    diagonal = jnp.concatenate([diagonal, diagonal], axis=1)
    packed[pl.ds(side, 8), :] = jnp.broadcast_to(diagonal, (8, univ))


def solve_kernel(scale, terms, *rest):
    packs, (field, basis, inverse) = rest[:terms], rest[terms:]
    univ = inverse.shape[0]
    side = univ // 2
    packed = packs[0][...]
    for pack in packs[1:]:
        packed += pack[...]
    packed *= scale
    row_ids = lax.broadcasted_iota(jnp.int32, (side, side), 0)
    column_ids = lax.broadcasted_iota(jnp.int32, (side, side), 1)
    mixed = packed[:side, :side]
    turned = mixed.T
    head = jnp.where(row_ids <= column_ids, mixed, turned)
    last = jnp.where(row_ids > column_ids, mixed, turned)
    diagonal = jnp.broadcast_to(packed[side : side + 1, :side], (side, side))
    last = jnp.where(row_ids == column_ids, diagonal, last)
    inverse[pl.ds(0, side), :] = jnp.concatenate([head, packed[:side, side:]], axis=1)
    inverse[pl.ds(side, side), :] = jnp.concatenate([last, last], axis=1)

    count = univ // ROWS
    shape = (ROWS, univ)
    row_ids = lax.broadcasted_iota(jnp.int32, shape, 0)
    column_ids = lax.broadcasted_iota(jnp.int32, shape, 1)
    held = [inverse[pl.ds(b * ROWS, ROWS), :] for b in range(count)]

    def spread(value, row):
        return jnp.broadcast_to(value[row : row + 1, :], shape)

    for b in range(count):
        rows = held[b]
        columns = [
            jnp.broadcast_to(rows[:, b * ROWS + j : b * ROWS + j + 1], shape) for j in range(ROWS)
        ]
        done = column_ids < (b + 1) * ROWS
        inside = done & (column_ids >= b * ROWS)
        rows = jnp.where(inside, jnp.where(column_ids == row_ids + b * ROWS, 1.0, 0.0), rows)
        pivots = jnp.ones(shape, jnp.float32)
        for j in range(ROWS):
            pivot = spread(columns[j], j)
            pivots = jnp.where(row_ids == j, pivot, pivots)
            if j < ROWS - 1:
                weight = jnp.where(row_ids > j, columns[j] * (1.0 / pivot), 0.0)
                for k in range(j + 1, ROWS):
                    columns[k] = columns[k] - weight * spread(columns[k], j)
                rows = rows - weight * spread(rows, j)
        inverse[pl.ds(b * ROWS, ROWS), :] = jnp.where(done, rows * lax.rsqrt(pivots), 0.0)
        if b < count - 1:
            turned = (rows * (1.0 / pivots)).T
            for c in range(b + 1, count):
                below = jnp.where(inside, 0.0, held[c])
                for j in range(ROWS):
                    weight = jnp.broadcast_to(turned[c * ROWS : (c + 1) * ROWS, j : j + 1], shape)
                    below = below - weight * spread(rows, j)
                held[c] = below
    inverse_high, inverse_low = split(inverse[...].T)
    wide = jnp.concatenate([inverse_high, inverse_low], axis=1)
    for image in range(field.shape[0]):
        high, low = split(field[image])
        products = jnp.dot(high, wide, preferred_element_type=jnp.float32)
        products = products[:, :univ] + products[:, univ:]
        basis[image] = products + jnp.dot(
            low, inverse_high, preferred_element_type=jnp.float32
        )


def shards(panels, blocks, pairs, counts):
    devices = lax.axis_size("img")
    own_index = lax.axis_index("img")
    member = own_index % GROUP
    img_dev, half, univ = panels.shape
    slots, keypts, cols = blocks.shape
    units = 2 * img_dev
    per = next(width for width in (8, 6, 4, 3, 2, 1) if slots % width == 0)
    place = jnp.stack([lax.axis_index("rep"), own_index]).astype(jnp.int32)
    anywhere = pl.BlockSpec(memory_space=pl.ANY)

    near, numbers = pl.pallas_call(
        start_kernel,
        in_specs=[VMEM] * 3,
        out_specs=[VMEM] * 2,
        out_shape=[
            jax.ShapeDtypeStruct(panels.shape, jnp.bfloat16),
            jax.ShapeDtypeStruct((8, slots), jnp.int32),
        ],
        compiler_params=SMALL,
        name="start",
    )(panels, pairs.T, counts.reshape(1, 1))
    far = exchanged(near, "rep", 1)
    bucket = 2 * (slots // BAND)
    *returns, members, units_of, firsts = pl.pallas_call(
        functools.partial(reverse_kernel, per, devices),
        in_specs=[anywhere] + [VMEM] * 2 + [anywhere],
        out_specs=[VMEM] * GROUP + [SMEM] * 3,
        out_shape=[jax.ShapeDtypeStruct((units, cols, univ), jnp.bfloat16)] * GROUP
        + [jax.ShapeDtypeStruct((GROUP * bucket + 1,), jnp.int32)] * 3,
        scratch_shapes=[
            pltpu.VMEM(blocks.shape, blocks.dtype),
            pltpu.VMEM((img_dev, univ, keypts), jnp.bfloat16),
            pltpu.VMEM((GROUP * units + 1, univ, cols), jnp.float32),
            pltpu.SemaphoreType.DMA((slots // per,)),
            pltpu.SMEM(numbers.shape, numbers.dtype),
            pltpu.SemaphoreType.DMA(()),
            pltpu.SMEM((GROUP,), jnp.int32),
        ],
        compiler_params=LIMIT,
        cost_estimate=SHORT,
        name="reverse",
    )(numbers, near, far, blocks)

    arrived = [exchanged(returns[bits], "img", bits) for bits in range(1, GROUP)]
    part = (img_dev, cols, univ)
    sums = [jnp.zeros(part, jnp.float32) for _ in range(3)]
    for bits, value in enumerate([returns[0]] + arrived):
        first_unit = value[:img_dev].astype(jnp.float32)
        second_unit = value[img_dev:].astype(jnp.float32)
        earlier = (member ^ bits) < member
        sums[0] += jnp.where(earlier, first_unit, 0)
        sums[1] += jnp.where(earlier, second_unit, first_unit)
        sums[2] += jnp.where(earlier, 0, second_unit)
    near_sum = sums[0]
    ahead_sums = [value.astype(jnp.bfloat16) for value in sums[1:]]
    back = [
        passed_along(value, "img", hop * GROUP) for hop, value in enumerate(ahead_sums, start=1)
    ]

    near_late = near
    ahead = [
        near,
        passed_along(near_late, "img", -GROUP),
        passed_along(near_late, "img", -2 * GROUP),
    ]
    *ahead, _ = lax.optimization_barrier((*ahead, returns[0]))
    tables = [jnp.concatenate(ahead[1:])]
    def forward_scratch(picked):
        return [
            pltpu.VMEM((len(picked) * bucket, keypts, cols), jnp.bfloat16),
            pltpu.VMEM((img_dev + 1, keypts, univ), jnp.float32),
            pltpu.SemaphoreType.DMA((len(picked) * bucket,)),
        ]

    before = pl.pallas_call(
        functools.partial(forward_first_kernel, (0,)),
        in_specs=[SMEM] * 3 + [anywhere, VMEM],
        out_specs=VMEM,
        out_shape=jax.ShapeDtypeStruct((img_dev, keypts, univ), jnp.float32),
        scratch_shapes=forward_scratch((0,)),
        compiler_params=LIMIT,
        cost_estimate=SHORT,
        name="forward_first",
    )(members, units_of, firsts, blocks, tables[0])
    for bits in range(1, GROUP):
        later = member > (member ^ bits)
        if bits == GROUP - 1:
            *ahead, before, arrived[1] = lax.optimization_barrier((*ahead, before, arrived[1]))
        sent = jnp.where(later, jnp.concatenate(ahead[:2]), jnp.concatenate(ahead[1:]))
        tables.append(exchanged(sent, "img", bits))

    middle, late = tuple(range(1, GROUP - 1)), (GROUP - 1,)
    before = pl.pallas_call(
        functools.partial(forward_next_kernel, middle),
        in_specs=[SMEM] * 3 + [anywhere] + [VMEM] * (1 + len(middle)),
        out_specs=VMEM,
        out_shape=jax.ShapeDtypeStruct((img_dev, keypts, univ), jnp.float32),
        scratch_shapes=forward_scratch(middle),
        compiler_params=LIMIT,
        cost_estimate=SHORT,
        name="forward_next",
    )(members, units_of, firsts, blocks, before, *[tables[index] for index in middle])
    last_tables = [tables[index] for index in late]
    last_tables, near_sum, back = lax.optimization_barrier((last_tables, near_sum, back))
    own, send = pl.pallas_call(
        functools.partial(forward_last_kernel, late),
        in_specs=[SMEM] * 4 + [anywhere] + [VMEM] * (2 + len(late)),
        out_specs=[VMEM] * 2,
        out_shape=[jax.ShapeDtypeStruct((img_dev, half, univ), jnp.float32)] * 2,
        scratch_shapes=forward_scratch(late),
        compiler_params=LIMIT,
        cost_estimate=SHORT,
        name="forward_last",
    )(place, members, units_of, firsts, blocks, panels, before, *last_tables)
    other_half = exchanged(send, "rep", 1)

    field, packed = pl.pallas_call(
        gram_kernel,
        in_specs=[VMEM] * 5,
        out_specs=[VMEM] * 2,
        out_shape=[
            jax.ShapeDtypeStruct(panels.shape, jnp.float32),
            jax.ShapeDtypeStruct((univ // 2 + 8, univ), jnp.float32),
        ],
        compiler_params=SMALL,
        name="gram",
    )(own, other_half, near_sum, *back)
    terms = [packed, exchanged(packed, "rep", 1)]
    bits = 1
    while bits < devices:
        packed = sum(terms)
        terms = [packed] + [exchanged(packed, "img", bits * k) for k in range(1, min(4, devices // bits))]
        bits *= 4
    return pl.pallas_call(
        functools.partial(solve_kernel, 1 / (devices * img_dev * keypts), len(terms)),
        in_specs=[VMEM] * (len(terms) + 1),
        out_specs=VMEM,
        out_shape=jax.ShapeDtypeStruct(panels.shape, jnp.float32),
        scratch_shapes=[pltpu.VMEM((univ, univ), jnp.float32)],
        compiler_params=SMALL,
        name="solve",
    )(*terms, field)


def solution(mesh):
    in_specs = (P("img", "rep", None), P("img", None, "rep"), P("img", None), P("img"))
    out_specs = P("img", "rep", None)
    return jax.shard_map(shards, mesh=mesh, in_specs=in_specs, out_specs=out_specs, check_vma=False)
```
